256 devices in a mesh: inp: 4 (over y_lo, core), tm: 64 (over z, y_hi, x).
Axes of the slice: x: 4, y: 4 (y_hi: 2, y_lo: 2; y = y_hi * 2 + y_lo), z: 8, core: 2. Of those that a mesh axis runs over, the one named last changes fastest.
Arguments:
- samples: bfloat16 [2, 2048, 262144], P(None, 'inp', 'tm'), may hold values from -6 to 6
- weights: bfloat16 [2, 2048, 256], P(None, 'inp'), may hold values from -0.09375 to 0.09375
- filter_taps: float32 [8, 1024], replicated, may hold values from -2 to 2
Outputs:
- spectrum: float32 [256, 256, 2, 1024], P('inp', 'tm')
The draws below stay inside these ranges and needn't reach their ends.
All inputs are finite; a program needn't handle non-finite values.
Results may differ from the reference program's by a relative error of at most 0.012.
Values may be sent and summed in bfloat16 or wider, within the bound.
A program may use at most 64 MiB of HBM per device.

```python
import jax
import jax.numpy as jnp
from jax import lax

INPUTS = 2048
BEAMS = 256
CHAN = 1024
TAPS = 8
FRAMES = 256
SAMPLES = 262144
N_INP = 4
N_TM = 64


def block_scale(rng, dims, pieces, low, largest):
    loudness, own = 1.0, jax.random.fold_in(rng, 6)
    for axis_at, parts in pieces:
        heights = jnp.exp(jax.random.uniform(jax.random.fold_in(own, axis_at), (parts,), jnp.float32, low / len(pieces), largest / len(pieces)))
        loudness = loudness * jnp.repeat(heights, dims[axis_at] // parts).reshape([-1 if axis == axis_at else 1 for axis in range(len(dims))])
    return loudness


def noise(key, dims, spread, limit, pieces=(), held_as=jnp.bfloat16):
    array = spread * jax.random.normal(key, dims, jnp.float32)
    if pieces:
        array = array * block_scale(key, dims, pieces, -0.22, 0.18)
    return jnp.clip(array, -limit, limit).astype(held_as)


def setup_inputs(seed: int = 0) -> dict:
    key_list = jax.random.split(jax.random.key(seed), 4)
    return {
        "samples": noise(key_list[0], (2, INPUTS, SAMPLES), 1.0, 6.0, ((1, 4), (2, 64))),
        "weights": noise(key_list[1], (2, INPUTS, BEAMS), (2 * INPUTS) ** -0.5, 0.09375, ((1, 4),)),
        "filter_taps": noise(key_list[2], (TAPS, CHAN), TAPS ** -0.5, 2.0, (), jnp.float32),
    }


def reference(samples, weights, filter_taps):
    weight_real = weights[0].astype(jnp.float32)
    weight_quad = weights[1].astype(jnp.float32)
    coupling = jnp.stack([jnp.stack([weight_real, -weight_quad]), jnp.stack([weight_quad, weight_real])])
    group_size = INPUTS // N_INP
    coupling = coupling.reshape(2, 2, N_INP, group_size, BEAMS)
    block_len = SAMPLES // N_TM

    def one_block(block_index):
        first = (block_index * block_len).astype(jnp.int32)
        columns = lax.dynamic_slice_in_dim(samples, first, block_len, 2).astype(jnp.float32)
        columns = columns.reshape(2, N_INP, group_size, block_len)
        partial_value = jnp.einsum('ocgib,cgit->gobt', coupling, columns)
        rounded = lax.optimization_barrier(partial_value.astype(jnp.bfloat16))
        return lax.optimization_barrier(jnp.sum(rounded.astype(jnp.float32), axis=0))
    blocks = lax.map(one_block, jnp.arange(N_TM, dtype=jnp.int32))
    beams = jnp.transpose(blocks, (1, 2, 0, 3)).reshape(2, BEAMS, SAMPLES)
    history = TAPS - 1
    padded = jnp.concatenate([jnp.zeros((2, BEAMS, history * CHAN), jnp.float32), beams], axis=2)
    framed = padded.reshape(2, BEAMS, FRAMES + history, CHAN)
    filtered = jnp.zeros((2, BEAMS, FRAMES, CHAN), jnp.float32)
    for tap_index in range(TAPS):
        filtered = filtered + filter_taps[tap_index] * framed[:, :, tap_index:tap_index + FRAMES]
    transformed = jnp.fft.fft(filtered[0] + 1j * filtered[1], axis=-1)
    norm_factor = 1.0 / jnp.sqrt(jnp.float32(CHAN))
    spectrum = jnp.stack([jnp.real(transformed), jnp.imag(transformed)], axis=2) * norm_factor
    return spectrum.astype(jnp.float32)
```

```python
import functools

import jax
import jax.numpy as jnp
import ml_dtypes
import numpy as np
from jax import lax
from jax.experimental import pallas as pl
from jax.experimental.pallas import tpu as pltpu
from jax.sharding import PartitionSpec as P

MESH = pl.DeviceIdType.MESH
LANES = 128
ROW_CHIPS = 4


def transform_table(channels):
    at = np.arange(channels, dtype=np.int64)
    angle = (at[:, None] * at[None, :] % channels) * (2.0 * np.pi / channels)
    cos = (np.cos(angle) / np.sqrt(channels)).reshape(-1, LANES, channels)
    sin = (np.sin(angle) / np.sqrt(channels)).reshape(-1, LANES, channels)
    return np.concatenate([cos, sin], axis=1).astype(ml_dtypes.bfloat16)


def kernel(
    steps,
    frames,
    x_hbm,
    w_hbm,
    taps,
    tab_hbm,
    out,
    xbuf,
    wbuf,
    steer,
    pbuf,
    rbuf,
    sbuf,
    ybuf,
    fbuf,
    pin,
    qin,
    ap,
    aq,
    bp,
    bq,
    tab,
    lhs,
    xsem,
    wsem,
    tsem,
    r1s,
    r1r,
    r2s,
    r2r,
    ps,
    pr,
    qs,
    qr,
    rps,
    rqs,
    aps,
    aqs,
    bps,
    bqs,
):
    i, t = lax.axis_index("inp"), lax.axis_index("tm")
    last = lax.axis_size("tm") - 1
    core = lax.rem(i, 2)
    lo = i // 2
    x = lax.rem(t, ROW_CHIPS)
    first_col, end_col = x == 0, x == ROW_CHIPS - 1
    has_prev, has_next = t > 0, t < last
    other_i = lo * 2 + (1 - core)
    pair_i = (1 - lo) * 2 + core
    sibling = {"inp": other_i, "tm": t}
    pair = {"inp": pair_i, "tm": t}
    nxt = {"inp": jnp.where(end_col, pair_i, i), "tm": jnp.where(has_next, t + 1, t)}
    prv = {"inp": jnp.where(first_col, pair_i, i), "tm": jnp.where(has_prev, t - 1, t)}
    depth = x_hbm.shape[1]
    channels = taps.shape[1]
    beams = fbuf.shape[1] // 2
    half = beams
    width = frames * LANES

    def load_x(c, f):
        return pltpu.make_async_copy(
            x_hbm.at[:, :, pl.ds(pl.multiple_of(f * channels + c * LANES, LANES), LANES)],
            xbuf.at[c, :, :, pl.ds(f * LANES, LANES)],
            xsem.at[c, f],
        )

    load_w = pltpu.make_async_copy(w_hbm, wbuf, wsem)
    load_t = pltpu.make_async_copy(tab_hbm, tab, tsem)
    load_w.start()
    for f in range(frames):
        load_x(0, f).start()

    barrier = pltpu.get_barrier_semaphore()
    pl.semaphore_signal(barrier, inc=1, device_id=sibling, device_id_type=MESH)
    pl.semaphore_signal(barrier, inc=1, device_id=pair, device_id_type=MESH)

    @pl.when(has_prev)
    def _():
        pl.semaphore_signal(barrier, inc=1, device_id=prv, device_id_type=MESH)

    def start_x(c, carry):
        for f in range(frames):
            load_x(c, f).start()
        return carry

    lax.fori_loop(1, steps, start_x, 0)
    load_t.start()
    load_w.wait()
    for block in range(4):
        to_core, to_lo = block // 2, block % 2
        first = (to_lo * 2 + to_core) * beams
        base = to_lo * 2 * beams
        re = wbuf[0, :, first : first + beams].astype(jnp.float32).T.astype(jnp.bfloat16)
        im = wbuf[1, :, first : first + beams].astype(jnp.float32).T.astype(jnp.bfloat16)
        steer[to_core, base : base + beams, :depth] = re
        steer[to_core, base : base + beams, depth:] = -im
        steer[to_core, base + beams : base + 2 * beams, :depth] = im
        steer[to_core, base + beams : base + 2 * beams, depth:] = re

    @pl.when(jnp.logical_not(has_prev))
    def _():
        pin[...] = jnp.zeros_like(pin)
        qin[...] = jnp.zeros_like(qin)

    pl.semaphore_wait(barrier, jnp.where(has_next, 3, 2))

    def remote(src, dst, send, recv, to):
        return pltpu.make_async_remote_copy(
            src_ref=src, dst_ref=dst, send_sem=send, recv_sem=recv, device_id=to, device_id_type=MESH
        )

    def to_sibling(c):
        return remote(pbuf.at[c, 1 - core], rbuf.at[c], r1s.at[c], r1r.at[c], sibling)

    def to_pair(c):
        return remote(sbuf.at[c], ybuf.at[c], r2s.at[c], r2r.at[c], pair)

    def part(ref, c, h):
        return ref.at[c, pl.ds(h * half, half)]

    def own_on(c, h):
        return remote(part(fbuf, c, h), part(pin, c, h), ps.at[c, h], pr.at[c, h], nxt)

    def own_up(c):
        return remote(part(fbuf, c, 0), ap.at[c], ps.at[c, 0], aps.at[c], nxt)

    def own_across(c):
        return remote(part(fbuf, c, 1), bp.at[c], ps.at[c, 1], bps.at[c], pair)

    def late(c, h):
        return pin.at[c, pl.ds(h * half, half), pl.ds(LANES, width - LANES)]

    def old_on(c, h):
        return remote(late(c, h), part(qin, c, h), qs.at[c, h], qr.at[c, h], nxt)

    def old_up(c):
        return remote(late(c, 0), aq.at[c], qs.at[c, 0], aqs.at[c], nxt)

    def old_across(c):
        return remote(late(c, 1), bq.at[c], qs.at[c, 1], bqs.at[c], pair)

    def own_relay_first(c):
        return remote(ap.at[c], part(pin, c, 0), rps.at[c], pr.at[c, 0], pair)

    def own_relay_end(c):
        return remote(bp.at[c], part(pin, c, 1), rps.at[c], pr.at[c, 1], nxt)

    def old_relay_first(c):
        return remote(aq.at[c], part(qin, c, 0), rqs.at[c], qr.at[c, 0], pair)

    def old_relay_end(c):
        return remote(bq.at[c], part(qin, c, 1), rqs.at[c], qr.at[c, 1], nxt)

    in_row = jnp.logical_and(has_next, jnp.logical_not(end_col))
    row_end = jnp.logical_and(has_next, end_col)
    row_start = jnp.logical_and(has_prev, first_col)

    def form(c):
        for f in range(frames):
            load_x(c, f).wait()
        xs = xbuf[c].reshape(2 * depth, width)
        pbuf[c, 1 - core] = jnp.dot(
            steer[1 - core], xs, preferred_element_type=jnp.float32
        ).astype(jnp.bfloat16).reshape(2, 2 * beams, width)
        to_sibling(c).start()
        pbuf[c, core] = jnp.dot(
            steer[core], xs, preferred_element_type=jnp.float32
        ).astype(jnp.bfloat16).reshape(2, 2 * beams, width)

    def gather_chip(c):
        to_sibling(c).wait_recv()
        total = pbuf[c, core, 1 - lo].astype(jnp.float32) + rbuf[c, 1 - lo].astype(jnp.float32)
        sbuf[c] = total.astype(jnp.bfloat16)
        to_pair(c).start()

    def gather_pair(c):
        to_pair(c).wait_recv()
        total = (
            pbuf[c, core, lo].astype(jnp.float32)
            + rbuf[c, lo].astype(jnp.float32)
            + ybuf[c].astype(jnp.float32)
        )
        fbuf[c] = total.astype(jnp.bfloat16)

        @pl.when(in_row)
        def _():
            own_on(c, 0).start()
            own_on(c, 1).start()

        @pl.when(row_end)
        def _():
            own_up(c).start()
            own_across(c).start()

    def relay_own(c):
        @pl.when(row_start)
        def _():
            own_up(c).wait_recv()
            own_relay_first(c).start()

        @pl.when(row_end)
        def _():
            own_across(c).wait_recv()
            own_relay_end(c).start()

    def pass_old(c):
        @pl.when(has_prev)
        def _():
            own_on(c, 0).wait_recv()
            own_on(c, 1).wait_recv()

        @pl.when(in_row)
        def _():
            old_on(c, 0).start()
            old_on(c, 1).start()

        @pl.when(row_end)
        def _():
            old_up(c).start()
            old_across(c).start()

    def relay_old(c):
        @pl.when(row_start)
        def _():
            old_up(c).wait_recv()
            old_relay_first(c).start()

        @pl.when(row_end)
        def _():
            old_across(c).wait_recv()
            old_relay_end(c).start()

    def finish(c):
        @pl.when(has_prev)
        def _():
            old_on(c, 0).wait_recv()
            old_on(c, 1).wait_recv()

        @pl.when(c == 0)
        def _():
            load_t.wait()

        weights = taps[:, pl.ds(pl.multiple_of(c * LANES, LANES), LANES)]
        count = weights.shape[0]
        for p in range(2):
            rows = slice(p * beams, (p + 1) * beams)
            window = []
            for f in range(frames - 1):
                window.append(qin[c, rows, f * LANES : (f + 1) * LANES].astype(jnp.float32))
            for f in range(frames):
                window.append(pin[c, rows, f * LANES : (f + 1) * LANES].astype(jnp.float32))
            for f in range(frames):
                window.append(fbuf[c, rows, f * LANES : (f + 1) * LANES].astype(jnp.float32))
            for j in range(frames):
                total = weights[0:1] * window[j]
                for k in range(1, count):
                    total = total + weights[k : k + 1] * window[j + k]
                at = slice(j * beams, (j + 1) * beams)
                below = slice((frames + j) * beams, (frames + j + 1) * beams)
                value = total.astype(jnp.bfloat16)
                lhs[at, p * LANES : (p + 1) * LANES] = value
                if p == 0:
                    lhs[below, LANES:] = -value
                else:
                    lhs[below, :LANES] = value
        pieces = out.shape[1] // 256
        for n in range(pieces):
            cols = slice(n * 256, (n + 1) * 256)
            piece = jnp.dot(lhs[...], tab[c, :, cols], preferred_element_type=jnp.float32)

            @pl.when(c == 0)
            def _():
                out[:, cols] = piece

            @pl.when(c > 0)
            def _():
                out[:, cols] += piece

    stages = [
        (0, form),
        (1, gather_chip),
        (2, gather_pair),
        (3, relay_own),
        (4, pass_old),
        (5, relay_old),
        (6, finish),
    ]

    def turn(k, carry):
        for lag, stage in stages:
            c = k - lag

            @pl.when(jnp.logical_and(c >= 0, c < steps))
            def _():
                stage(c)

        return carry

    lax.fori_loop(0, steps + stages[-1][0], turn, 0)

    def drain(c, carry):
        to_sibling(c).wait_send()
        to_pair(c).wait_send()

        @pl.when(has_next)
        def _():
            for h in range(2):
                own_on(c, h).wait_send()
                old_on(c, h).wait_send()

        @pl.when(jnp.logical_or(row_start, row_end))
        def _():
            own_relay_first(c).wait_send()
            old_relay_first(c).wait_send()

        return carry

    lax.fori_loop(0, steps, drain, 0)


def body(samples, weights, filter_taps):
    depth, span = samples.shape[1:]
    owned = weights.shape[2] // lax.axis_size("inp")
    channels = filter_taps.shape[1]
    frames = span // channels
    steps = channels // LANES
    width = frames * LANES
    table = jnp.asarray(transform_table(channels))
    half = jnp.bfloat16
    dma = pltpu.SemaphoreType.DMA
    rows = 2 * owned
    anywhere = pl.BlockSpec(memory_space=pl.ANY)
    inside = pl.BlockSpec(memory_space=pltpu.VMEM)
    spectrum = pl.pallas_call(
        functools.partial(kernel, steps, frames),
        out_shape=jax.ShapeDtypeStruct((2 * frames * owned, channels), jnp.float32),
        in_specs=[anywhere, anywhere, inside, anywhere],
        out_specs=inside,
        scratch_shapes=[
            pltpu.VMEM((steps, 2, depth, width), half),
            pltpu.VMEM(weights.shape, half),
            pltpu.VMEM((2, 2 * rows, 2 * depth), half),
            pltpu.VMEM((steps, 2, 2, rows, width), half),
            pltpu.VMEM((steps, 2, rows, width), half),
            pltpu.VMEM((steps, rows, width), half),
            pltpu.VMEM((steps, rows, width), half),
            pltpu.VMEM((steps, rows, width), half),
            pltpu.VMEM((steps, rows, width), half),
            pltpu.VMEM((steps, rows, width - LANES), half),
            pltpu.VMEM((steps, owned, width), half),
            pltpu.VMEM((steps, owned, width - LANES), half),
            pltpu.VMEM((steps, owned, width), half),
            pltpu.VMEM((steps, owned, width - LANES), half),
            pltpu.VMEM(table.shape, half),
            pltpu.VMEM((2 * frames * owned, 2 * LANES), half),
            dma((steps, frames)),
            dma,
            dma,
            dma((steps,)),
            dma((steps,)),
            dma((steps,)),
            dma((steps,)),
            dma((steps, 2)),
            dma((steps, 2)),
            dma((steps, 2)),
            dma((steps, 2)),
            dma((steps,)),
            dma((steps,)),
            dma((steps,)),
            dma((steps,)),
            dma((steps,)),
            dma((steps,)),
        ],
        compiler_params=pltpu.CompilerParams(
            collective_id=0, has_side_effects=True, vmem_limit_bytes=52 << 20
        ),
        name="beams",
    )(samples, weights, filter_taps, table)
    return spectrum.reshape(2, frames, owned, channels).transpose(2, 1, 0, 3)


def solution(mesh):
    return jax.shard_map(
        body,
        mesh=mesh,
        in_specs=(P(None, "inp", "tm"), P(None, "inp", None), P()),
        out_specs=P("inp", "tm", None, None),
        check_vma=False,
    )
```

```python
import functools

import jax
import jax.numpy as jnp
import ml_dtypes
import numpy as np
from jax import lax
from jax.experimental import pallas as pl
from jax.experimental.pallas import tpu as pltpu
from jax.sharding import PartitionSpec as P

MESH = pl.DeviceIdType.MESH
LANES = 128
ROW_CHIPS = 4
LEFT_FRAMES = 2


def transform_table(channels):
    at = np.arange(channels, dtype=np.int64)
    angle = (at[:, None] * at[None, :] % channels) * (2.0 * np.pi / channels)
    cos = (np.cos(angle) / np.sqrt(channels)).reshape(-1, LANES, channels)
    sin = (np.sin(angle) / np.sqrt(channels)).reshape(-1, LANES, channels)
    return np.concatenate([cos, sin], axis=1).astype(ml_dtypes.bfloat16)


def kernel(
    steps,
    frames,
    x_hbm,
    w_hbm,
    taps_hbm,
    tab_hbm,
    out,
    xbuf,
    wbuf,
    taps,
    tab,
    steer,
    pbuf,
    rbuf,
    sbuf,
    ybuf,
    fbuf,
    pin,
    qin,
    lbuf,
    cbuf,
    gbuf,
    gmid,
    base,
    lhs,
    xsem,
    wsem,
    ksem,
    tsem,
    r1s,
    r1r,
    r2s,
    r2r,
    ps,
    pr,
    qs,
    qr,
    ls,
    lr,
    ms,
    cs,
    cr,
    ds,
    gs,
    gr,
    hs,
):
    i, t = lax.axis_index("inp"), lax.axis_index("tm")
    row_count = lax.axis_size("tm") // ROW_CHIPS
    core = lax.rem(i, 2)
    lo = i // 2
    x = lax.rem(t, ROW_CHIPS)
    row = t // ROW_CHIPS
    row_prev, row_next = row > 0, row < row_count - 1
    other_i = lo * 2 + (1 - core)
    pair_i = (1 - lo) * 2 + core
    sibling = {"inp": other_i, "tm": t}
    pair = {"inp": pair_i, "tm": t}
    back, on = ROW_CHIPS - 1, ROW_CHIPS - 1

    def near(by):
        return {"inp": i, "tm": t + by}

    def cross(by):
        return {"inp": pair_i, "tm": t + by}

    at0, at1, at2, at3 = x == 0, x == 1, x == 2, x == 3
    inner = x < 3
    row_end = jnp.logical_and(at3, row_next)
    row_start = jnp.logical_and(at0, row_prev)
    lead = jnp.logical_and(at2, row_next)
    trail = jnp.logical_and(at2, row_prev)
    fed = jnp.logical_and(at1, row_prev)

    depth = x_hbm.shape[1]
    channels = taps.shape[1]
    count = taps.shape[0]
    beams = fbuf.shape[1] // 2
    half = beams
    width = frames * LANES
    by_left = lbuf.shape[2]

    def load_x(c, f):
        return pltpu.make_async_copy(
            x_hbm.at[:, :, pl.ds(pl.multiple_of(f * channels + c * LANES, LANES), LANES)],
            xbuf.at[c, :, :, pl.ds(f * LANES, LANES)],
            xsem.at[c, f],
        )

    load_w = pltpu.make_async_copy(w_hbm, wbuf, wsem)
    load_k = pltpu.make_async_copy(taps_hbm, taps, ksem)
    load_t = pltpu.make_async_copy(tab_hbm, tab, tsem)
    load_w.start()
    for f in range(frames):
        load_x(0, f).start()

    barrier = pltpu.get_barrier_semaphore()

    def greet(device):
        pl.semaphore_signal(barrier, inc=1, device_id=device, device_id_type=MESH)

    greet(sibling)
    greet(pair)

    @pl.when(at0)
    def _():
        greet(near(1))

    @pl.when(row_start)
    def _():
        greet(cross(-1))

    @pl.when(at1)
    def _():
        greet(near(-1))

    @pl.when(fed)
    def _():
        greet(cross(-back))
        greet(cross(1))

    @pl.when(at2)
    def _():
        greet(near(-1))
        greet(near(1))

    @pl.when(lead)
    def _():
        greet(cross(1))

    @pl.when(trail)
    def _():
        greet(cross(-back))

    @pl.when(at3)
    def _():
        greet(near(-1))
        greet(near(-back))

    def start_x(c, carry):
        for f in range(frames):
            load_x(c, f).start()
        return carry

    lax.fori_loop(1, steps, start_x, 0)
    load_k.start()
    load_t.start()
    load_w.wait()
    for block in range(4):
        to_core, to_lo = block // 2, block % 2
        first = (to_lo * 2 + to_core) * beams
        top = to_lo * 2 * beams
        re = wbuf[0, :, first : first + beams].astype(jnp.float32).T.astype(jnp.bfloat16)
        im = wbuf[1, :, first : first + beams].astype(jnp.float32).T.astype(jnp.bfloat16)
        steer[to_core, top : top + beams, :depth] = re
        steer[to_core, top : top + beams, depth:] = -im
        steer[to_core, top + beams : top + 2 * beams, :depth] = im
        steer[to_core, top + beams : top + 2 * beams, depth:] = re

    @pl.when(jnp.logical_not(row_prev))
    def _():
        @pl.when(at0)
        def _():
            pin[...] = jnp.zeros_like(pin)

        @pl.when(at1)
        def _():
            qin[...] = jnp.zeros_like(qin)

    one = jnp.int32(1)
    ahead = jnp.where(row_next, one, 0)
    behind = jnp.where(row_prev, one, 0)
    sends = jnp.where(x < 2, 2, jnp.where(at2, 1 + ahead + behind, 1 + 3 * ahead))
    pl.semaphore_wait(barrier, 2 + sends)

    def remote(src, dst, send, recv, to):
        return pltpu.make_async_remote_copy(
            src_ref=src, dst_ref=dst, send_sem=send, recv_sem=recv, device_id=to, device_id_type=MESH
        )

    def to_sibling(c):
        return remote(pbuf.at[c, 1 - core], rbuf.at[c], r1s.at[c], r1r.at[c], sibling)

    def to_pair(c):
        return remote(sbuf.at[c], ybuf.at[c], r2s.at[c], r2r.at[c], pair)

    def rows(ref, c, h):
        return ref.at[c, pl.ds(h * half, half)]

    def own_on(c):
        return remote(fbuf.at[c], pin.at[c], ps.at[c], pr.at[c, 0], near(1))

    def own_left(c):
        src = fbuf.at[c, :, pl.ds(LANES, by_left)]
        to = {"inp": i, "tm": jnp.where(at0, t + on, t - 1)}
        return remote(src, lbuf.at[c], ls.at[c], lr.at[c], to)

    def left_on(c):
        to = {"inp": i, "tm": jnp.where(at0, t + on, t - 1)}
        return remote(lbuf.at[c], qin.at[c, :, pl.ds(0, by_left)], ms.at[c], qr.at[c, 0], to)

    def old_on(c):
        keep = width - LANES - by_left
        src = pin.at[c, :, pl.ds(LANES + by_left, keep)]
        return remote(src, qin.at[c, :, pl.ds(by_left, keep)], qs.at[c], qr.at[c, 1], near(1))

    def row_old(c, h):
        src = fbuf.at[c, pl.ds(h * half, half), pl.ds(LANES, width - LANES)]
        to = cross(-1) if h == 0 else cross(on)
        return remote(src, cbuf.at[c, h], cs.at[c, h], cr.at[c, h], to)

    def row_old_on(c, h):
        to = cross(on) if h == 0 else cross(-1)
        return remote(cbuf.at[c, h], rows(qin, c, h), ds.at[c, h], qr.at[c, h], to)

    def ahead_up(c, h):
        to = cross(1) if h == 0 else pair
        return remote(rows(gbuf, c, h), gmid.at[c], gs.at[c, h], gr.at[c], to)

    def ahead_on(c):
        h = jnp.where(at0, 0, 1)
        to = {"inp": pair_i, "tm": jnp.where(at0, t, t + 1)}
        dst = pin.at[c, pl.ds(pl.multiple_of(h * half, half), half)]
        return remote(gmid.at[c], dst, hs.at[c], pr.at[c, h], to)

    def ahead_in(c, h):
        return remote(gmid.at[c], rows(pin, c, h), hs.at[c], pr.at[c, h], pair)

    def form(c):
        for f in range(frames):
            load_x(c, f).wait()
        xs = xbuf[c].reshape(2 * depth, width)
        pbuf[c, 1 - core] = jnp.dot(
            steer[1 - core], xs, preferred_element_type=jnp.float32
        ).astype(jnp.bfloat16).reshape(2, 2 * beams, width)
        to_sibling(c).start()
        pbuf[c, core] = jnp.dot(
            steer[core], xs, preferred_element_type=jnp.float32
        ).astype(jnp.bfloat16).reshape(2, 2 * beams, width)

    def gather_chip(c):
        to_sibling(c).wait_recv()
        total = pbuf[c, core, 1 - lo].astype(jnp.float32) + rbuf[c, 1 - lo].astype(jnp.float32)
        sbuf[c] = total.astype(jnp.bfloat16)
        to_pair(c).start()

    def gather_pair(c):
        to_pair(c).wait_recv()
        total = (
            pbuf[c, core, lo].astype(jnp.float32)
            + rbuf[c, lo].astype(jnp.float32)
            + ybuf[c].astype(jnp.float32)
        )
        fbuf[c] = total.astype(jnp.bfloat16)

        @pl.when(inner)
        def _():
            own_on(c).start()

        @pl.when(x < 2)
        def _():
            own_left(c).start()

        @pl.when(row_end)
        def _():
            row_old(c, 0).start()
            row_old(c, 1).start()

    def chunk_taps(c):
        return taps[:, pl.ds(pl.multiple_of(c * LANES, LANES), LANES)]

    def frame(ref, c, at, f):
        return ref[c, at, f * LANES : (f + 1) * LANES].astype(jnp.float32)

    def pass_on(c):
        @pl.when(x > 0)
        def _():
            own_on(c).wait_recv()

        @pl.when(jnp.logical_or(at1, at2))
        def _():
            old_on(c).start()

        @pl.when(row_end)
        def _():
            weights = chunk_taps(c)
            for h in range(2):
                at = slice(h * half, (h + 1) * half)
                window = [frame(pin, c, at, f) for f in range(1, frames)]
                window += [frame(fbuf, c, at, f) for f in range(frames)]
                for j in range(frames):
                    total = weights[0:1] * window[j]
                    for k in range(1, count - 1 - j):
                        total = total + weights[k : k + 1] * window[j + k]
                    gbuf[c, at, j * LANES : (j + 1) * LANES] = total.astype(jnp.bfloat16)
                ahead_up(c, h).start()

    def relay_old(c):
        @pl.when(lead)
        def _():
            row_old(c, 0).wait_recv()
            row_old_on(c, 0).start()

        @pl.when(trail)
        def _():
            row_old(c, 1).wait_recv()
            row_old_on(c, 1).start()

        @pl.when(jnp.logical_or(at0, at3))
        def _():
            own_left(c).wait_recv()
            left_on(c).start()

    def relay_ahead(c):
        @pl.when(jnp.logical_or(row_start, row_end))
        def _():
            ahead_up(c, 0).wait_recv()
            ahead_on(c).start()

    def finish(c):
        @pl.when(row_start)
        def _():
            ahead_in(c, 0).wait_recv()
            ahead_in(c, 1).wait_recv()

        @pl.when(fed)
        def _():
            row_old_on(c, 0).wait_recv()
            row_old_on(c, 1).wait_recv()

        @pl.when(x > 1)
        def _():
            left_on(c).wait_recv()
            old_on(c).wait_recv()

        @pl.when(c == 0)
        def _():
            load_t.wait()

        weights = chunk_taps(c)

        @pl.when(at0)
        def _():
            base[...] = pin[c].astype(jnp.float32)

        @pl.when(x > 0)
        def _():
            for p in range(2):
                at = slice(p * beams, (p + 1) * beams)
                window = [frame(qin, c, at, f) for f in range(frames - 1)]
                window += [frame(pin, c, at, f) for f in range(frames)]
                for j in range(frames):
                    total = weights[0:1] * window[j]
                    for k in range(1, count - 1 - j):
                        total = total + weights[k : k + 1] * window[j + k]
                    base[at, j * LANES : (j + 1) * LANES] = total

        for p in range(2):
            at = slice(p * beams, (p + 1) * beams)
            window = [frame(fbuf, c, at, f) for f in range(frames)]
            for j in range(frames):
                total = base[at, j * LANES : (j + 1) * LANES]
                for f in range(j + 1):
                    k = count - 1 - j + f
                    total = total + weights[k : k + 1] * window[f]
                above = slice(j * beams, (j + 1) * beams)
                below = slice((frames + j) * beams, (frames + j + 1) * beams)
                value = total.astype(jnp.bfloat16)
                lhs[above, p * LANES : (p + 1) * LANES] = value
                if p == 0:
                    lhs[below, LANES:] = -value
                else:
                    lhs[below, :LANES] = value
        for n in range(channels // 256):
            cols = slice(n * 256, (n + 1) * 256)
            piece = jnp.dot(lhs[...], tab[c, :, cols], preferred_element_type=jnp.float32)

            @pl.when(c == 0)
            def _():
                out[:, cols] = piece

            @pl.when(c > 0)
            def _():
                out[:, cols] += piece

    stages = [
        (0, form),
        (1, gather_chip),
        (2, gather_pair),
        (3, pass_on),
        (3, relay_old),
        (4, relay_ahead),
        (5, finish),
    ]
    load_k.wait()

    def turn(k, carry):
        for lag, stage in stages:
            c = k - lag

            @pl.when(jnp.logical_and(c >= 0, c < steps))
            def _():
                stage(c)

        return carry

    lax.fori_loop(0, steps + stages[-1][0], turn, 0)

    def drain(c, carry):
        to_sibling(c).wait_send()
        to_pair(c).wait_send()

        @pl.when(inner)
        def _():
            own_on(c).wait_send()

        @pl.when(x < 2)
        def _():
            own_left(c).wait_send()

        @pl.when(jnp.logical_or(at0, at3))
        def _():
            left_on(c).wait_send()

        @pl.when(jnp.logical_or(at1, at2))
        def _():
            old_on(c).wait_send()

        @pl.when(row_end)
        def _():
            for h in range(2):
                row_old(c, h).wait_send()
                ahead_up(c, h).wait_send()

        @pl.when(lead)
        def _():
            row_old_on(c, 0).wait_send()

        @pl.when(trail)
        def _():
            row_old_on(c, 1).wait_send()

        @pl.when(jnp.logical_or(row_start, row_end))
        def _():
            ahead_on(c).wait_send()

        return carry

    lax.fori_loop(0, steps, drain, 0)


def spread(rows, out, sem):
    owned, frames = out.shape[:2]
    copies = []
    for part in range(2):
        for f in range(frames):
            at = (part * frames + f) * owned
            copies.append(
                pltpu.make_async_copy(rows.at[pl.ds(at, owned)], out.at[:, f, part], sem.at[part, f])
            )
    for copy in copies:
        copy.start()
    for copy in copies:
        copy.wait()


def body(samples, weights, filter_taps):
    depth, span = samples.shape[1:]
    owned = weights.shape[2] // lax.axis_size("inp")
    channels = filter_taps.shape[1]
    frames = span // channels
    steps = channels // LANES
    width = frames * LANES
    old = width - LANES
    table = jnp.asarray(transform_table(channels))
    half = jnp.bfloat16
    dma = pltpu.SemaphoreType.DMA
    rows = 2 * owned
    anywhere = pl.BlockSpec(memory_space=pltpu.HBM)
    inside = pl.BlockSpec(memory_space=pltpu.VMEM)
    one, two = dma((steps,)), dma((steps, 2))
    lines = pl.pallas_call(
        functools.partial(kernel, steps, frames),
        out_shape=jax.ShapeDtypeStruct((2 * frames * owned, channels), jnp.float32),
        in_specs=[anywhere] * 4,
        out_specs=inside,
        scratch_shapes=[
            pltpu.VMEM((steps, 2, depth, width), half),
            pltpu.VMEM(weights.shape, half),
            pltpu.VMEM(filter_taps.shape, jnp.float32),
            pltpu.VMEM(table.shape, half),
            pltpu.VMEM((2, 2 * rows, 2 * depth), half),
            pltpu.VMEM((steps, 2, 2, rows, width), half),
            pltpu.VMEM((steps, 2, rows, width), half),
            pltpu.VMEM((steps, rows, width), half),
            pltpu.VMEM((steps, rows, width), half),
            pltpu.VMEM((steps, rows, width), half),
            pltpu.VMEM((steps, rows, width), half),
            pltpu.VMEM((steps, rows, old), half),
            pltpu.VMEM((steps, rows, LEFT_FRAMES * LANES), half),
            pltpu.VMEM((steps, 2, owned, old), half),
            pltpu.VMEM((steps, rows, width), half),
            pltpu.VMEM((steps, owned, width), half),
            pltpu.VMEM((rows, width), jnp.float32),
            pltpu.VMEM((2 * frames * owned, 2 * LANES), half),
            dma((steps, frames)),
            dma,
            dma,
            dma,
            one,
            one,
            one,
            one,
            one,
            two,
            one,
            two,
            one,
            one,
            one,
            two,
            two,
            two,
            two,
            one,
            one,
        ],
        compiler_params=pltpu.CompilerParams(
            collective_id=0, has_side_effects=True, vmem_limit_bytes=61 << 20
        ),
        name="beams",
    )(samples, weights, filter_taps, table)
    return pl.pallas_call(
        spread,
        out_shape=jax.ShapeDtypeStruct((owned, frames, 2, channels), jnp.float32),
        in_specs=[inside],
        out_specs=pl.BlockSpec(memory_space=pltpu.HBM),
        scratch_shapes=[dma((2, frames))],
        name="spread",
    )(lines)


def solution(mesh):
    return jax.shard_map(
        body,
        mesh=mesh,
        in_specs=(P(None, "inp", "tm"), P(None, "inp", None), P()),
        out_specs=P("inp", "tm", None, None),
        check_vma=False,
    )
```

```python
import functools

import jax
import jax.numpy as jnp
import ml_dtypes
import numpy as np
from jax import lax
from jax.experimental import pallas as pl
from jax.experimental.pallas import tpu as pltpu
from jax.sharding import PartitionSpec as P

MESH = pl.DeviceIdType.MESH
LANES = 128
ROW_CHIPS = 4
AHEAD = 2
RIGHT = 1
DRAIN_LAG = 14


def transform_table(channels):
    at = np.arange(channels, dtype=np.int64)
    angle = (at[:, None] * at[None, :] % channels) * (2.0 * np.pi / channels)
    cos = (np.cos(angle) / np.sqrt(channels)).reshape(-1, LANES, channels)
    sin = (np.sin(angle) / np.sqrt(channels)).reshape(-1, LANES, channels)
    return np.concatenate([cos, sin], axis=1).astype(ml_dtypes.bfloat16)


def kernel(
    steps,
    frames,
    x_hbm,
    w_hbm,
    taps_hbm,
    tab_hbm,
    out,
    xbuf,
    wbuf,
    taps,
    tab,
    steer,
    pbuf,
    rbuf,
    sbuf,
    ybuf,
    fbuf,
    pin,
    qin,
    lbuf,
    cbuf,
    gbuf,
    gmid,
    base,
    lhs,
    xsem,
    wsem,
    ksem,
    tsem,
    r1s,
    r1r,
    r2s,
    r2r,
    ps,
    pr,
    qs,
    qr,
    ls,
    lr,
    ms,
    cs,
    cr,
    ds,
    gs,
    gr,
    hs,
):
    i, t = lax.axis_index("inp"), lax.axis_index("tm")
    row_count = lax.axis_size("tm") // ROW_CHIPS
    core = lax.rem(i, 2)
    lo = i // 2
    x = lax.rem(t, ROW_CHIPS)
    row = t // ROW_CHIPS
    row_prev, row_next = row > 0, row < row_count - 1
    other_i = lo * 2 + (1 - core)
    pair_i = (1 - lo) * 2 + core
    sibling = {"inp": other_i, "tm": t}
    pair = {"inp": pair_i, "tm": t}
    back, on = ROW_CHIPS - 1, ROW_CHIPS - 1

    def near(by):
        return {"inp": i, "tm": t + by}

    def cross(by):
        return {"inp": pair_i, "tm": t + by}

    at0, at1, at2, at3 = x == 0, x == 1, x == 2, x == 3
    inner = x < 3
    row_end = jnp.logical_and(at3, row_next)
    row_start = jnp.logical_and(at0, row_prev)
    lead = jnp.logical_and(at2, row_next)
    trail = jnp.logical_and(at2, row_prev)
    fed = jnp.logical_and(at1, row_prev)

    depth = x_hbm.shape[1]
    channels = taps.shape[1]
    count = taps.shape[0]
    part_rows = fbuf.shape[1] // 2
    beams = 2 * part_rows
    width = frames * LANES

    def load_x(c, f):
        return pltpu.make_async_copy(
            x_hbm.at[:, :, pl.ds(pl.multiple_of(f * channels + c * LANES, LANES), LANES)],
            xbuf.at[c, :, :, pl.ds(f * LANES, LANES)],
            xsem.at[c, f],
        )

    load_w = pltpu.make_async_copy(w_hbm, wbuf, wsem)
    load_k = pltpu.make_async_copy(taps_hbm, taps, ksem)
    load_t = pltpu.make_async_copy(tab_hbm, tab, tsem)
    load_w.start()
    for f in range(frames):
        load_x(0, f).start()

    barrier = pltpu.get_barrier_semaphore()

    def greet(device):
        pl.semaphore_signal(barrier, inc=1, device_id=device, device_id_type=MESH)

    greet(sibling)
    greet(pair)

    @pl.when(at0)
    def _():
        greet(near(1))

    @pl.when(row_start)
    def _():
        greet(cross(-1))

    @pl.when(at1)
    def _():
        greet(near(-1))

    @pl.when(fed)
    def _():
        greet(cross(-back))
        greet(cross(1))

    @pl.when(at2)
    def _():
        greet(near(-1))
        greet(near(1))

    @pl.when(lead)
    def _():
        greet(cross(1))

    @pl.when(trail)
    def _():
        greet(cross(-back))

    @pl.when(at3)
    def _():
        greet(near(-1))
        greet(near(-back))

    def start_x(c, carry):
        for f in range(frames):
            load_x(c, f).start()
        return carry

    lax.fori_loop(1, AHEAD, start_x, 0)
    load_k.start()
    load_w.wait()
    real, imag = wbuf[0].T, wbuf[1].T
    for block in range(8):
        to_core, h, to_lo = block // 4, block // 2 % 2, block % 2
        first = (to_lo * 2 + to_core) * beams + h * part_rows
        top = (h * 2 + to_lo) * beams
        mid, end = top + part_rows, top + 2 * part_rows
        re, im = real[first : first + part_rows], imag[first : first + part_rows]
        steer[to_core, top:mid, :depth] = re
        steer[to_core, top:mid, depth:] = -im
        steer[to_core, mid:end, :depth] = im
        steer[to_core, mid:end, depth:] = re

    @pl.when(jnp.logical_not(row_prev))
    def _():
        @pl.when(at0)
        def _():
            pin[...] = jnp.zeros_like(pin)

        @pl.when(at1)
        def _():
            qin[...] = jnp.zeros_like(qin)

    one = jnp.int32(1)
    ahead = jnp.where(row_next, one, 0)
    behind = jnp.where(row_prev, one, 0)
    sends = jnp.where(x < 2, 2, jnp.where(at2, 1 + ahead + behind, 1 + 3 * ahead))
    pl.semaphore_wait(barrier, 2 + sends)

    def remote(src, dst, send, recv, to):
        return pltpu.make_async_remote_copy(
            src_ref=src, dst_ref=dst, send_sem=send, recv_sem=recv, device_id=to, device_id_type=MESH
        )

    def to_sibling(s):
        return remote(pbuf.at[s, 1 - core], rbuf.at[s], r1s.at[s], r1r.at[s], sibling)

    def to_pair(s):
        return remote(sbuf.at[s], ybuf.at[s], r2s.at[s], r2r.at[s], pair)

    def own_on(s):
        return remote(fbuf.at[s], pin.at[s], ps.at[s], pr.at[s], near(1))

    def old_on(s):
        src = pin.at[s, :, pl.ds(LANES, width - LANES)]
        return remote(src, qin.at[s], qs.at[s], qr.at[s], near(1))

    def own_old(s):
        return fbuf.at[s, :, pl.ds(LANES, width - LANES)]

    def left():
        return {"inp": i, "tm": jnp.where(at0, t + on, t - 1)}

    def own_left(s):
        return remote(own_old(s), lbuf.at[s], ls.at[s], lr.at[s], left())

    def left_on(s):
        return remote(lbuf.at[s], qin.at[s], ms.at[s], qr.at[s], left())

    def row_old(s, h):
        to = cross(-1) if h == 0 else cross(on)
        return remote(own_old(s), cbuf.at[s], cs.at[s], cr.at[s], to)

    def row_old_on(s, h):
        to = cross(on) if h == 0 else cross(-1)
        return remote(cbuf.at[s], qin.at[s], ds.at[s], qr.at[s], to)

    def ahead_up(s, h):
        to = cross(1) if h == 0 else pair
        return remote(gbuf.at[s], gmid.at[s], gs.at[s], gr.at[s], to)

    def ahead_on(s, h):
        to = pair if h == 0 else cross(1)
        return remote(gmid.at[s], pin.at[s], hs.at[s], pr.at[s], to)

    def goes_left(s):
        return lax.rem(s, 4) >= RIGHT

    def relays_old(h):
        return lead if h == 0 else trail

    def relays_ahead(h):
        return row_start if h == 0 else row_end

    def form(s, h):
        if h == 1:
            return
        c = s // 2

        @pl.when(c + AHEAD < steps)
        def _():
            start_x(c + AHEAD, 0)

        @pl.when(c == AHEAD)
        def _():
            load_t.start()

        for f in range(frames):
            load_x(c, f).wait()
        xs = xbuf[c].reshape(2 * depth, width)
        for to_core in (1 - core, core):
            value = jnp.dot(steer[to_core], xs, preferred_element_type=jnp.float32)
            value = value.astype(jnp.bfloat16).reshape(2, 2, beams, width)
            for g in range(2):
                pbuf[s + g, to_core] = value[g]
                if to_core is not core:
                    to_sibling(s + g).start()

    def gather_chip(s, h):
        to_sibling(s).wait_recv()
        total = pbuf[s, core, 1 - lo].astype(jnp.float32) + rbuf[s, 1 - lo].astype(jnp.float32)
        sbuf[s] = total.astype(jnp.bfloat16)
        to_pair(s).start()

    def gather_pair(s, h):
        to_pair(s).wait_recv()
        total = (
            pbuf[s, core, lo].astype(jnp.float32)
            + rbuf[s, lo].astype(jnp.float32)
            + ybuf[s].astype(jnp.float32)
        )
        fbuf[s] = total.astype(jnp.bfloat16)

        @pl.when(inner)
        def _():
            own_on(s).start()

        @pl.when(jnp.logical_and(x < 2, goes_left(s)))
        def _():
            own_left(s).start()

        @pl.when(row_end)
        def _():
            row_old(s, h).start()

    def chunk_taps(s):
        return taps[:, pl.ds(pl.multiple_of(s // 2 * LANES, LANES), LANES)]

    def frame(ref, s, at, f):
        return ref[s, at, f * LANES : (f + 1) * LANES].astype(jnp.float32)

    def pass_on(s, h):
        @pl.when(x > 0)
        def _():
            own_on(s).wait_recv()

        @pl.when(jnp.logical_and(jnp.logical_or(at1, at2), jnp.logical_not(goes_left(s))))
        def _():
            old_on(s).start()

        @pl.when(row_end)
        def _():
            weights = chunk_taps(s)
            at = slice(0, 2 * part_rows)
            window = [frame(pin, s, at, f) for f in range(1, frames)]
            window += [frame(fbuf, s, at, f) for f in range(frames)]
            for j in range(frames):
                total = weights[0:1] * window[j]
                for k in range(1, count - 1 - j):
                    total = total + weights[k : k + 1] * window[j + k]
                gbuf[s, at, j * LANES : (j + 1) * LANES] = total.astype(jnp.bfloat16)
            ahead_up(s, h).start()

    def relay_old(s, h):
        @pl.when(relays_old(h))
        def _():
            row_old(s, h).wait_recv()
            row_old_on(s, h).start()

        @pl.when(jnp.logical_and(jnp.logical_or(at0, at3), goes_left(s)))
        def _():
            own_left(s).wait_recv()
            left_on(s).start()

    def relay_ahead(s, h):
        @pl.when(relays_ahead(h))
        def _():
            ahead_up(s, h).wait_recv()
            ahead_on(s, h).start()

    def finish(s, h):
        @pl.when(row_start)
        def _():
            ahead_on(s, h).wait_recv()

        @pl.when(jnp.logical_or(fed, x > 1))
        def _():
            old_on(s).wait_recv()

        if h == 0:

            @pl.when(s == 0)
            def _():
                load_t.wait()

        weights = chunk_taps(s)

        @pl.when(at0)
        def _():
            base[...] = pin[s].astype(jnp.float32)

        @pl.when(x > 0)
        def _():
            at = slice(0, 2 * part_rows)
            window = [frame(qin, s, at, f) for f in range(frames - 1)]
            window += [frame(pin, s, at, f) for f in range(frames)]
            for j in range(frames):
                total = weights[0:1] * window[j]
                for k in range(1, count - 1 - j):
                    total = total + weights[k : k + 1] * window[j + k]
                base[at, j * LANES : (j + 1) * LANES] = total

        for p in range(2):
            at = slice(p * part_rows, (p + 1) * part_rows)
            window = [frame(fbuf, s, at, f) for f in range(frames)]
            for j in range(frames):
                total = base[at, j * LANES : (j + 1) * LANES]
                for f in range(j + 1):
                    k = count - 1 - j + f
                    total = total + weights[k : k + 1] * window[f]
                above = slice(j * part_rows, (j + 1) * part_rows)
                below = slice((frames + j) * part_rows, (frames + j + 1) * part_rows)
                value = total.astype(jnp.bfloat16)
                lhs[above, p * LANES : (p + 1) * LANES] = value
                if p == 0:
                    lhs[below, LANES:] = -value
                else:
                    lhs[below, :LANES] = value
        lines = slice(h * 2 * frames * part_rows, (h + 1) * 2 * frames * part_rows)
        for n in range(channels // 256):
            cols = slice(n * 256, (n + 1) * 256)
            piece = jnp.dot(lhs[...], tab[s // 2, :, cols], preferred_element_type=jnp.float32)

            @pl.when(s < 2)
            def _():
                out[lines, cols] = piece

            @pl.when(s >= 2)
            def _():
                out[lines, cols] += piece

    def drain(s, h):
        to_sibling(s).wait_send()
        to_pair(s).wait_send()

        @pl.when(inner)
        def _():
            own_on(s).wait_send()

        @pl.when(row_end)
        def _():
            row_old(s, h).wait_send()
            ahead_up(s, h).wait_send()

        @pl.when(relays_old(h))
        def _():
            row_old_on(s, h).wait_send()

        @pl.when(relays_ahead(h))
        def _():
            ahead_on(s, h).wait_send()

        @pl.when(jnp.logical_and(x < 2, goes_left(s)))
        def _():
            own_left(s).wait_send()

        @pl.when(jnp.logical_and(jnp.logical_or(at0, at3), goes_left(s)))
        def _():
            left_on(s).wait_send()

        @pl.when(jnp.logical_and(jnp.logical_or(at1, at2), jnp.logical_not(goes_left(s))))
        def _():
            old_on(s).wait_send()

    stages = [
        (0, form),
        (1, gather_chip),
        (3, gather_pair),
        (5, pass_on),
        (5, relay_old),
        (7, relay_ahead),
        (DRAIN_LAG, drain),
        (9, finish),
    ]
    load_k.wait()

    def turn(k, carry):
        for now in range(2):
            for lag, stage in stages:
                s = 2 * k + now - lag

                @pl.when(jnp.logical_and(s >= 0, s < 2 * steps))
                def _():
                    stage(s, (now - lag) % 2)

        return carry

    turns = steps + (stages[-1][0] + 1) // 2
    lax.fori_loop(0, turns, turn, 0)

    def settle(c, carry):
        for h in range(2):
            drain(2 * c + h, h)
        return carry

    lax.fori_loop((turns * 2 - DRAIN_LAG) // 2, steps, settle, 0)


def spread(rows, out, sem):
    owned, frames = out.shape[:2]
    half = owned // 2
    copies = []
    for h in range(2):
        for part in range(2):
            for f in range(frames):
                at = ((h * 2 + part) * frames + f) * half
                to = out.at[pl.ds(h * half, half), f, part]
                copies.append(
                    pltpu.make_async_copy(rows.at[pl.ds(at, half)], to, sem.at[h, part, f])
                )
    for copy in copies:
        copy.start()
    for copy in copies:
        copy.wait()


def body(samples, weights, filter_taps):
    depth, span = samples.shape[1:]
    owned = weights.shape[2] // lax.axis_size("inp")
    channels = filter_taps.shape[1]
    frames = span // channels
    steps = channels // LANES
    width = frames * LANES
    old = width - LANES
    table = jnp.asarray(transform_table(channels))
    half = jnp.bfloat16
    dma = pltpu.SemaphoreType.DMA
    rows = 2 * owned
    units = 2 * steps
    anywhere = pl.BlockSpec(memory_space=pltpu.HBM)
    inside = pl.BlockSpec(memory_space=pltpu.VMEM)
    lines = pl.pallas_call(
        functools.partial(kernel, steps, frames),
        out_shape=jax.ShapeDtypeStruct((2 * frames * owned, channels), jnp.float32),
        in_specs=[anywhere] * 4,
        out_specs=inside,
        scratch_shapes=[
            pltpu.VMEM((steps, 2, depth, width), half),
            pltpu.VMEM(weights.shape, half),
            pltpu.VMEM(filter_taps.shape, jnp.float32),
            pltpu.VMEM(table.shape, half),
            pltpu.VMEM((2, 2 * rows, 2 * depth), half),
            pltpu.VMEM((units, 2, 2, owned, width), half),
            pltpu.VMEM((units, 2, owned, width), half),
            pltpu.VMEM((units, owned, width), half),
            pltpu.VMEM((units, owned, width), half),
            pltpu.VMEM((units, owned, width), half),
            pltpu.VMEM((units, owned, width), half),
            pltpu.VMEM((units, owned, old), half),
            pltpu.VMEM((units, owned, old), half),
            pltpu.VMEM((units, owned, old), half),
            pltpu.VMEM((units, owned, width), half),
            pltpu.VMEM((units, owned, width), half),
            pltpu.VMEM((owned, width), jnp.float32),
            pltpu.VMEM((frames * owned, 2 * LANES), half),
            dma((steps, frames)),
            dma,
            dma,
            dma,
            dma((units,)),
            dma((units,)),
            dma((units,)),
            dma((units,)),
            dma((units,)),
            dma((units,)),
            dma((units,)),
            dma((units,)),
            dma((units,)),
            dma((units,)),
            dma((units,)),
            dma((units,)),
            dma((units,)),
            dma((units,)),
            dma((units,)),
            dma((units,)),
            dma((units,)),
        ],
        compiler_params=pltpu.CompilerParams(
            collective_id=0, has_side_effects=True, vmem_limit_bytes=61 << 20
        ),
        name="beams",
    )(samples, weights, filter_taps, table)
    return pl.pallas_call(
        spread,
        out_shape=jax.ShapeDtypeStruct((owned, frames, 2, channels), jnp.float32),
        in_specs=[inside],
        out_specs=pl.BlockSpec(memory_space=pltpu.HBM),
        scratch_shapes=[dma((2, 2, frames))],
        name="spread",
    )(lines)


def solution(mesh):
    return jax.shard_map(
        body,
        mesh=mesh,
        in_specs=(P(None, "inp", "tm"), P(None, "inp", None), P()),
        out_specs=P("inp", "tm", None, None),
        check_vma=False,
    )
```

```python
import functools

import jax
import jax.numpy as jnp
import ml_dtypes
import numpy as np
from jax import lax
from jax.experimental import pallas as pl
from jax.experimental.pallas import tpu as pltpu
from jax.sharding import PartitionSpec as P

MESH = pl.DeviceIdType.MESH
LANES = 128
ROW_CHIPS = 4
AHEAD = 2
RIGHT = 1
DRAIN_LAG = 14


def transform_table(channels):
    at = np.arange(channels, dtype=np.int64)
    angle = (at[:, None] * at[None, :] % channels) * (2.0 * np.pi / channels)
    cos = (np.cos(angle) / np.sqrt(channels)).reshape(-1, LANES, channels)
    sin = (np.sin(angle) / np.sqrt(channels)).reshape(-1, LANES, channels)
    return np.concatenate([cos, sin], axis=1).astype(ml_dtypes.bfloat16)


def kernel(
    steps,
    frames,
    x_hbm,
    w_hbm,
    taps_hbm,
    tab_hbm,
    out,
    xbuf,
    wbuf,
    taps,
    tab,
    steer,
    pbuf,
    rbuf,
    sbuf,
    ybuf,
    fbuf,
    pin,
    qin,
    lbuf,
    cbuf,
    gbuf,
    gmid,
    base,
    lhs,
    xsem,
    wsem,
    ksem,
    tsem,
    r1s,
    r1r,
    r2s,
    r2r,
    ps,
    pr,
    qs,
    qr,
    ls,
    lr,
    ms,
    cs,
    cr,
    ds,
    gs,
    gr,
    hs,
):
    i, t = lax.axis_index("inp"), lax.axis_index("tm")
    row_count = lax.axis_size("tm") // ROW_CHIPS
    core = lax.rem(i, 2)
    lo = i // 2
    x = lax.rem(t, ROW_CHIPS)
    row = t // ROW_CHIPS
    row_prev, row_next = row > 0, row < row_count - 1
    other_i = lo * 2 + (1 - core)
    pair_i = (1 - lo) * 2 + core
    sibling = {"inp": other_i, "tm": t}
    pair = {"inp": pair_i, "tm": t}
    back, on = ROW_CHIPS - 1, ROW_CHIPS - 1

    def near(by):
        return {"inp": i, "tm": t + by}

    def cross(by):
        return {"inp": pair_i, "tm": t + by}

    at0, at1, at2, at3 = x == 0, x == 1, x == 2, x == 3
    inner = x < 3
    row_end = jnp.logical_and(at3, row_next)
    row_start = jnp.logical_and(at0, row_prev)
    lead = jnp.logical_and(at2, row_next)
    trail = jnp.logical_and(at2, row_prev)
    fed = jnp.logical_and(at1, row_prev)

    depth = x_hbm.shape[1]
    channels = taps.shape[1]
    count = taps.shape[0]
    part_rows = fbuf.shape[1] // 2
    beams = 2 * part_rows
    width = frames * LANES

    def load_x(c, f):
        return pltpu.make_async_copy(
            x_hbm.at[:, :, pl.ds(pl.multiple_of(f * channels + c * LANES, LANES), LANES)],
            xbuf.at[c, :, :, pl.ds(f * LANES, LANES)],
            xsem.at[c, f],
        )

    load_w = pltpu.make_async_copy(w_hbm, wbuf, wsem)
    load_k = pltpu.make_async_copy(taps_hbm, taps, ksem)
    load_t = pltpu.make_async_copy(tab_hbm, tab, tsem)
    load_w.start()
    for f in range(frames):
        load_x(0, f).start()

    barrier = pltpu.get_barrier_semaphore()

    def greet(device):
        pl.semaphore_signal(barrier, inc=1, device_id=device, device_id_type=MESH)

    greet(sibling)
    greet(pair)

    @pl.when(at0)
    def _():
        greet(near(1))

    @pl.when(row_start)
    def _():
        greet(cross(-1))

    @pl.when(at1)
    def _():
        greet(near(-1))

    @pl.when(fed)
    def _():
        greet(cross(-back))
        greet(cross(1))

    @pl.when(at2)
    def _():
        greet(near(-1))
        greet(near(1))

    @pl.when(lead)
    def _():
        greet(cross(1))

    @pl.when(trail)
    def _():
        greet(cross(-back))

    @pl.when(at3)
    def _():
        greet(near(-1))
        greet(near(-back))

    def start_x(c, carry):
        for f in range(frames):
            load_x(c, f).start()
        return carry

    lax.fori_loop(1, AHEAD, start_x, 0)
    load_k.start()
    load_w.wait()
    real, imag = wbuf[0].T, wbuf[1].T
    for block in range(8):
        to_core, h, to_lo = block // 4, block // 2 % 2, block % 2
        first = (to_lo * 2 + to_core) * beams + h * part_rows
        top = (h * 2 + to_lo) * beams
        mid, end = top + part_rows, top + 2 * part_rows
        re, im = real[first : first + part_rows], imag[first : first + part_rows]
        steer[to_core, top:mid, :depth] = re
        steer[to_core, top:mid, depth:] = -im
        steer[to_core, mid:end, :depth] = im
        steer[to_core, mid:end, depth:] = re

    @pl.when(jnp.logical_not(row_prev))
    def _():
        @pl.when(at0)
        def _():
            pin[...] = jnp.zeros_like(pin)

        @pl.when(at1)
        def _():
            qin[...] = jnp.zeros_like(qin)

    def multiply(c, to_core):
        xs = xbuf[c].reshape(2 * depth, width)
        value = jnp.dot(steer[to_core], xs, preferred_element_type=jnp.float32)
        value = value.astype(jnp.bfloat16).reshape(2, 2, beams, width)
        pbuf[2 * c, to_core] = value[0]
        pbuf[2 * c + 1, to_core] = value[1]

    for f in range(frames):
        load_x(0, f).wait()
    multiply(0, 1 - core)
    multiply(0, core)

    one = jnp.int32(1)
    ahead = jnp.where(row_next, one, 0)
    behind = jnp.where(row_prev, one, 0)
    sends = jnp.where(x < 2, 2, jnp.where(at2, 1 + ahead + behind, 1 + 3 * ahead))
    pl.semaphore_wait(barrier, 2 + sends)

    def remote(src, dst, send, recv, to):
        return pltpu.make_async_remote_copy(
            src_ref=src, dst_ref=dst, send_sem=send, recv_sem=recv, device_id=to, device_id_type=MESH
        )

    def to_sibling(s):
        return remote(pbuf.at[s, 1 - core], rbuf.at[s], r1s.at[s], r1r.at[s], sibling)

    def to_pair(s):
        return remote(sbuf.at[s], ybuf.at[s], r2s.at[s], r2r.at[s], pair)

    def own_on(s):
        return remote(fbuf.at[s], pin.at[s], ps.at[s], pr.at[s], near(1))

    def old_on(s):
        src = pin.at[s, :, pl.ds(LANES, width - LANES)]
        return remote(src, qin.at[s], qs.at[s], qr.at[s], near(1))

    def own_old(s):
        return fbuf.at[s, :, pl.ds(LANES, width - LANES)]

    def left():
        return {"inp": i, "tm": jnp.where(at0, t + on, t - 1)}

    def own_left(s):
        return remote(own_old(s), lbuf.at[s], ls.at[s], lr.at[s], left())

    def left_on(s):
        return remote(lbuf.at[s], qin.at[s], ms.at[s], qr.at[s], left())

    def row_old(s, h):
        to = cross(-1) if h == 0 else cross(on)
        return remote(own_old(s), cbuf.at[s], cs.at[s], cr.at[s], to)

    def row_old_on(s, h):
        to = cross(on) if h == 0 else cross(-1)
        return remote(cbuf.at[s], qin.at[s], ds.at[s], qr.at[s], to)

    def ahead_up(s, h):
        to = cross(1) if h == 0 else pair
        return remote(gbuf.at[s], gmid.at[s], gs.at[s], gr.at[s], to)

    def ahead_on(s, h):
        to = pair if h == 0 else cross(1)
        return remote(gmid.at[s], pin.at[s], hs.at[s], pr.at[s], to)

    def goes_left(s):
        return lax.rem(s, 4) >= RIGHT

    def relays_old(h):
        return lead if h == 0 else trail

    def relays_ahead(h):
        return row_start if h == 0 else row_end

    def form(s, h):
        if h == 1:
            return
        c = s // 2

        @pl.when(c + AHEAD < steps)
        def _():
            start_x(c + AHEAD, 0)

        @pl.when(c == AHEAD)
        def _():
            load_t.start()

        @pl.when(c > 0)
        def _():
            for f in range(frames):
                load_x(c, f).wait()
            multiply(c, 1 - core)

        to_sibling(s).start()
        to_sibling(s + 1).start()

        @pl.when(c > 0)
        def _():
            multiply(c, core)

    def gather_chip(s, h):
        to_sibling(s).wait_recv()
        total = pbuf[s, core, 1 - lo].astype(jnp.float32) + rbuf[s, 1 - lo].astype(jnp.float32)
        sbuf[s] = total.astype(jnp.bfloat16)
        to_pair(s).start()

    def gather_pair(s, h):
        to_pair(s).wait_recv()
        total = (
            pbuf[s, core, lo].astype(jnp.float32)
            + rbuf[s, lo].astype(jnp.float32)
            + ybuf[s].astype(jnp.float32)
        )
        fbuf[s] = total.astype(jnp.bfloat16)

        @pl.when(inner)
        def _():
            own_on(s).start()

        @pl.when(jnp.logical_and(x < 2, goes_left(s)))
        def _():
            own_left(s).start()

        @pl.when(row_end)
        def _():
            row_old(s, h).start()

    def chunk_taps(s):
        return taps[:, pl.ds(pl.multiple_of(s // 2 * LANES, LANES), LANES)]

    def frame(ref, s, at, f):
        return ref[s, at, f * LANES : (f + 1) * LANES].astype(jnp.float32)

    def pass_on(s, h):
        @pl.when(x > 0)
        def _():
            own_on(s).wait_recv()

        @pl.when(jnp.logical_and(jnp.logical_or(at1, at2), jnp.logical_not(goes_left(s))))
        def _():
            old_on(s).start()

        @pl.when(row_end)
        def _():
            weights = chunk_taps(s)
            at = slice(0, 2 * part_rows)
            window = [frame(pin, s, at, f) for f in range(1, frames)]
            window += [frame(fbuf, s, at, f) for f in range(frames)]
            for j in range(frames):
                total = weights[0:1] * window[j]
                for k in range(1, count - 1 - j):
                    total = total + weights[k : k + 1] * window[j + k]
                gbuf[s, at, j * LANES : (j + 1) * LANES] = total.astype(jnp.bfloat16)
            ahead_up(s, h).start()

    def relay_old(s, h):
        @pl.when(relays_old(h))
        def _():
            row_old(s, h).wait_recv()
            row_old_on(s, h).start()

        @pl.when(jnp.logical_and(jnp.logical_or(at0, at3), goes_left(s)))
        def _():
            own_left(s).wait_recv()
            left_on(s).start()

    def relay_ahead(s, h):
        @pl.when(relays_ahead(h))
        def _():
            ahead_up(s, h).wait_recv()
            ahead_on(s, h).start()

    def finish(s, h):
        @pl.when(row_start)
        def _():
            ahead_on(s, h).wait_recv()

        @pl.when(jnp.logical_or(fed, x > 1))
        def _():
            old_on(s).wait_recv()

        if h == 0:

            @pl.when(s == 0)
            def _():
                load_t.wait()

        weights = chunk_taps(s)

        @pl.when(at0)
        def _():
            base[...] = pin[s].astype(jnp.float32)

        @pl.when(x > 0)
        def _():
            at = slice(0, 2 * part_rows)
            window = [frame(qin, s, at, f) for f in range(frames - 1)]
            window += [frame(pin, s, at, f) for f in range(frames)]
            for j in range(frames):
                total = weights[0:1] * window[j]
                for k in range(1, count - 1 - j):
                    total = total + weights[k : k + 1] * window[j + k]
                base[at, j * LANES : (j + 1) * LANES] = total

        for p in range(2):
            at = slice(p * part_rows, (p + 1) * part_rows)
            window = [frame(fbuf, s, at, f) for f in range(frames)]
            for j in range(frames):
                total = base[at, j * LANES : (j + 1) * LANES]
                for f in range(j + 1):
                    k = count - 1 - j + f
                    total = total + weights[k : k + 1] * window[f]
                above = slice(j * part_rows, (j + 1) * part_rows)
                below = slice((frames + j) * part_rows, (frames + j + 1) * part_rows)
                value = total.astype(jnp.bfloat16)
                lhs[above, p * LANES : (p + 1) * LANES] = value
                if p == 0:
                    lhs[below, LANES:] = -value
                else:
                    lhs[below, :LANES] = value
        lines = slice(h * 2 * frames * part_rows, (h + 1) * 2 * frames * part_rows)
        for n in range(channels // 256):
            cols = slice(n * 256, (n + 1) * 256)
            piece = jnp.dot(lhs[...], tab[s // 2, :, cols], preferred_element_type=jnp.float32)

            @pl.when(s < 2)
            def _():
                out[lines, cols] = piece

            @pl.when(s >= 2)
            def _():
                out[lines, cols] += piece

    def drain(s, h):
        to_sibling(s).wait_send()
        to_pair(s).wait_send()

        @pl.when(inner)
        def _():
            own_on(s).wait_send()

        @pl.when(row_end)
        def _():
            row_old(s, h).wait_send()
            ahead_up(s, h).wait_send()

        @pl.when(relays_old(h))
        def _():
            row_old_on(s, h).wait_send()

        @pl.when(relays_ahead(h))
        def _():
            ahead_on(s, h).wait_send()

        @pl.when(jnp.logical_and(x < 2, goes_left(s)))
        def _():
            own_left(s).wait_send()

        @pl.when(jnp.logical_and(jnp.logical_or(at0, at3), goes_left(s)))
        def _():
            left_on(s).wait_send()

        @pl.when(jnp.logical_and(jnp.logical_or(at1, at2), jnp.logical_not(goes_left(s))))
        def _():
            old_on(s).wait_send()

    stages = [
        (0, form),
        (1, gather_chip),
        (3, gather_pair),
        (5, pass_on),
        (6, relay_old),
        (7, relay_ahead),
        (DRAIN_LAG, drain),
        (9, finish),
    ]
    load_k.wait()

    def turn(k, carry):
        for now in range(2):
            for lag, stage in stages:
                s = 2 * k + now - lag

                @pl.when(jnp.logical_and(s >= 0, s < 2 * steps))
                def _():
                    stage(s, (now - lag) % 2)

        return carry

    turns = steps + (stages[-1][0] + 1) // 2
    lax.fori_loop(0, turns, turn, 0)

    def settle(c, carry):
        for h in range(2):
            drain(2 * c + h, h)
        return carry

    lax.fori_loop((turns * 2 - DRAIN_LAG) // 2, steps, settle, 0)


def spread(rows, out, sem):
    owned, frames = out.shape[:2]
    half = owned // 2
    copies = []
    for h in range(2):
        for part in range(2):
            for f in range(frames):
                at = ((h * 2 + part) * frames + f) * half
                to = out.at[pl.ds(h * half, half), f, part]
                copies.append(
                    pltpu.make_async_copy(rows.at[pl.ds(at, half)], to, sem.at[h, part, f])
                )
    for copy in copies:
        copy.start()
    for copy in copies:
        copy.wait()


def body(samples, weights, filter_taps):
    depth, span = samples.shape[1:]
    owned = weights.shape[2] // lax.axis_size("inp")
    channels = filter_taps.shape[1]
    frames = span // channels
    steps = channels // LANES
    width = frames * LANES
    old = width - LANES
    table = jnp.asarray(transform_table(channels))
    half = jnp.bfloat16
    dma = pltpu.SemaphoreType.DMA
    rows = 2 * owned
    units = 2 * steps
    anywhere = pl.BlockSpec(memory_space=pltpu.HBM)
    inside = pl.BlockSpec(memory_space=pltpu.VMEM)
    lines = pl.pallas_call(
        functools.partial(kernel, steps, frames),
        out_shape=jax.ShapeDtypeStruct((2 * frames * owned, channels), jnp.float32),
        in_specs=[anywhere] * 4,
        out_specs=inside,
        scratch_shapes=[
            pltpu.VMEM((steps, 2, depth, width), half),
            pltpu.VMEM(weights.shape, half),
            pltpu.VMEM(filter_taps.shape, jnp.float32),
            pltpu.VMEM(table.shape, half),
            pltpu.VMEM((2, 2 * rows, 2 * depth), half),
            pltpu.VMEM((units, 2, 2, owned, width), half),
            pltpu.VMEM((units, 2, owned, width), half),
            pltpu.VMEM((units, owned, width), half),
            pltpu.VMEM((units, owned, width), half),
            pltpu.VMEM((units, owned, width), half),
            pltpu.VMEM((units, owned, width), half),
            pltpu.VMEM((units, owned, old), half),
            pltpu.VMEM((units, owned, old), half),
            pltpu.VMEM((units, owned, old), half),
            pltpu.VMEM((units, owned, width), half),
            pltpu.VMEM((units, owned, width), half),
            pltpu.VMEM((owned, width), jnp.float32),
            pltpu.VMEM((frames * owned, 2 * LANES), half),
            dma((steps, frames)),
            dma,
            dma,
            dma,
            dma((units,)),
            dma((units,)),
            dma((units,)),
            dma((units,)),
            dma((units,)),
            dma((units,)),
            dma((units,)),
            dma((units,)),
            dma((units,)),
            dma((units,)),
            dma((units,)),
            dma((units,)),
            dma((units,)),
            dma((units,)),
            dma((units,)),
            dma((units,)),
            dma((units,)),
        ],
        compiler_params=pltpu.CompilerParams(
            collective_id=0, has_side_effects=True, vmem_limit_bytes=61 << 20
        ),
        name="beams",
    )(samples, weights, filter_taps, table)
    return pl.pallas_call(
        spread,
        out_shape=jax.ShapeDtypeStruct((owned, frames, 2, channels), jnp.float32),
        in_specs=[inside],
        out_specs=pl.BlockSpec(memory_space=pltpu.HBM),
        scratch_shapes=[dma((2, 2, frames))],
        name="spread",
    )(lines)


def solution(mesh):
    return jax.shard_map(
        body,
        mesh=mesh,
        in_specs=(P(None, "inp", "tm"), P(None, "inp", None), P()),
        out_specs=P("inp", "tm", None, None),
        check_vma=False,
    )
```

```python
import functools

import jax
import jax.numpy as jnp
import ml_dtypes
import numpy as np
from jax import lax
from jax.experimental import pallas as pl
from jax.experimental.pallas import tpu as pltpu
from jax.sharding import PartitionSpec as P

MESH = pl.DeviceIdType.MESH
LANES = 128
ROW_CHIPS = 4
AHEAD = 2
RIGHT = 1
DRAIN_LAG = 14


def transform_table(channels):
    at = np.arange(channels, dtype=np.int64)
    angle = (at[:, None] * at[None, :] % channels) * (2.0 * np.pi / channels)
    cos = (np.cos(angle) / np.sqrt(channels)).reshape(-1, LANES, channels)
    sin = (np.sin(angle) / np.sqrt(channels)).reshape(-1, LANES, channels)
    return np.concatenate([cos, sin], axis=1).astype(ml_dtypes.bfloat16)


def kernel(
    steps,
    frames,
    x_hbm,
    w_hbm,
    taps_hbm,
    tab_hbm,
    out,
    xbuf,
    wbuf,
    taps,
    tab,
    steer,
    pbuf,
    rbuf,
    sbuf,
    ybuf,
    fbuf,
    pin,
    qin,
    lbuf,
    cbuf,
    gbuf,
    gmid,
    base,
    lhs,
    xsem,
    wsem,
    ksem,
    tsem,
    r1s,
    r1r,
    r2s,
    r2r,
    ps,
    pr,
    qs,
    qr,
    ls,
    lr,
    ms,
    cs,
    cr,
    ds,
    gs,
    gr,
    hs,
):
    i, t = lax.axis_index("inp"), lax.axis_index("tm")
    row_count = lax.axis_size("tm") // ROW_CHIPS
    core = lax.rem(i, 2)
    lo = i // 2
    x = lax.rem(t, ROW_CHIPS)
    row = t // ROW_CHIPS
    row_prev, row_next = row > 0, row < row_count - 1
    other_i = lo * 2 + (1 - core)
    pair_i = (1 - lo) * 2 + core
    sibling = {"inp": other_i, "tm": t}
    pair = {"inp": pair_i, "tm": t}
    back, on = ROW_CHIPS - 1, ROW_CHIPS - 1

    def near(by):
        return {"inp": i, "tm": t + by}

    def cross(by):
        return {"inp": pair_i, "tm": t + by}

    at0, at1, at2, at3 = x == 0, x == 1, x == 2, x == 3
    inner = x < 3
    row_end = jnp.logical_and(at3, row_next)
    row_start = jnp.logical_and(at0, row_prev)
    lead = jnp.logical_and(at2, row_next)
    trail = jnp.logical_and(at2, row_prev)
    fed = jnp.logical_and(at1, row_prev)

    depth = x_hbm.shape[1]
    channels = taps.shape[1]
    count = taps.shape[0]
    part_rows = fbuf.shape[1] // 2
    beams = 2 * part_rows
    width = frames * LANES

    def load_x(c, f):
        return pltpu.make_async_copy(
            x_hbm.at[:, :, pl.ds(pl.multiple_of(f * channels + c * LANES, LANES), LANES)],
            xbuf.at[c, :, :, pl.ds(f * LANES, LANES)],
            xsem.at[c, f],
        )

    load_w = pltpu.make_async_copy(w_hbm, wbuf, wsem)
    load_k = pltpu.make_async_copy(taps_hbm, taps, ksem)
    load_t = pltpu.make_async_copy(tab_hbm, tab, tsem)
    load_w.start()
    for f in range(frames):
        load_x(0, f).start()

    barrier = pltpu.get_barrier_semaphore()

    def greet(device):
        pl.semaphore_signal(barrier, inc=1, device_id=device, device_id_type=MESH)

    greet(sibling)
    greet(pair)

    @pl.when(at0)
    def _():
        greet(near(1))

    @pl.when(row_start)
    def _():
        greet(cross(-1))

    @pl.when(at1)
    def _():
        greet(near(-1))

    @pl.when(fed)
    def _():
        greet(cross(-back))
        greet(cross(1))

    @pl.when(at2)
    def _():
        greet(near(-1))
        greet(near(1))

    @pl.when(lead)
    def _():
        greet(cross(1))

    @pl.when(trail)
    def _():
        greet(cross(-back))

    @pl.when(at3)
    def _():
        greet(near(-1))
        greet(near(-back))

    def start_x(c, carry):
        for f in range(frames):
            load_x(c, f).start()
        return carry

    lax.fori_loop(1, AHEAD, start_x, 0)
    load_k.start()
    load_w.wait()
    real, imag = wbuf[0].T, wbuf[1].T
    for block in range(8):
        to_core, h, to_lo = block // 4, block // 2 % 2, block % 2
        first = (to_lo * 2 + to_core) * beams + h * part_rows
        top = (h * 2 + to_lo) * beams
        mid, end = top + part_rows, top + 2 * part_rows
        re, im = real[first : first + part_rows], imag[first : first + part_rows]
        steer[to_core, top:mid, :depth] = re
        steer[to_core, top:mid, depth:] = -im
        steer[to_core, mid:end, :depth] = im
        steer[to_core, mid:end, depth:] = re

    @pl.when(jnp.logical_not(row_prev))
    def _():
        @pl.when(at0)
        def _():
            pin[...] = jnp.zeros_like(pin)

        @pl.when(at1)
        def _():
            qin[...] = jnp.zeros_like(qin)

    def multiply(c, to_core):
        xs = xbuf[c].reshape(2 * depth, width)
        value = jnp.dot(steer[to_core], xs, preferred_element_type=jnp.float32)
        value = value.astype(jnp.bfloat16).reshape(2, 2, beams, width)
        pbuf[2 * c, to_core] = value[0]
        pbuf[2 * c + 1, to_core] = value[1]

    for f in range(frames):
        load_x(0, f).wait()
    multiply(0, 1 - core)
    multiply(0, core)

    one = jnp.int32(1)
    ahead = jnp.where(row_next, one, 0)
    behind = jnp.where(row_prev, one, 0)
    sends = jnp.where(x < 2, 2, jnp.where(at2, 1 + ahead + behind, 1 + 3 * ahead))
    pl.semaphore_wait(barrier, 2 + sends)

    def remote(src, dst, send, recv, to):
        return pltpu.make_async_remote_copy(
            src_ref=src, dst_ref=dst, send_sem=send, recv_sem=recv, device_id=to, device_id_type=MESH
        )

    def to_sibling(s):
        return remote(pbuf.at[s, 1 - core], rbuf.at[s], r1s.at[s], r1r.at[s], sibling)

    def to_pair(s):
        return remote(sbuf.at[s], ybuf.at[s], r2s.at[s], r2r.at[s], pair)

    def own_on(s):
        return remote(fbuf.at[s], pin.at[s], ps.at[s], pr.at[s], near(1))

    def old_on(s):
        src = pin.at[s, :, pl.ds(LANES, width - LANES)]
        return remote(src, qin.at[s], qs.at[s], qr.at[s], near(1))

    def own_old(s):
        return fbuf.at[s, :, pl.ds(LANES, width - LANES)]

    def left():
        return {"inp": i, "tm": jnp.where(at0, t + on, t - 1)}

    def own_left(s):
        return remote(own_old(s), lbuf.at[s], ls.at[s], lr.at[s], left())

    def left_on(s):
        return remote(lbuf.at[s], qin.at[s], ms.at[s], qr.at[s], left())

    def row_old(s, h):
        to = cross(-1) if h == 0 else cross(on)
        return remote(own_old(s), cbuf.at[s], cs.at[s], cr.at[s], to)

    def row_old_on(s, h):
        to = cross(on) if h == 0 else cross(-1)
        return remote(cbuf.at[s], qin.at[s], ds.at[s], qr.at[s], to)

    def ahead_up(s, h):
        to = cross(1) if h == 0 else pair
        return remote(gbuf.at[s], gmid.at[s], gs.at[s], gr.at[s], to)

    def ahead_on(s, h):
        to = pair if h == 0 else cross(1)
        return remote(gmid.at[s], pin.at[s], hs.at[s], pr.at[s], to)

    def goes_left(s):
        return lax.rem(s, 3) >= RIGHT

    def relays_old(h):
        return lead if h == 0 else trail

    def relays_ahead(h):
        return row_start if h == 0 else row_end

    def form(s, h):
        if h == 1:
            return
        c = s // 2

        @pl.when(c + AHEAD < steps)
        def _():
            start_x(c + AHEAD, 0)

        @pl.when(c == AHEAD)
        def _():
            load_t.start()

        @pl.when(c > 0)
        def _():
            for f in range(frames):
                load_x(c, f).wait()
            multiply(c, 1 - core)

        to_sibling(s).start()
        to_sibling(s + 1).start()

        @pl.when(c > 0)
        def _():
            multiply(c, core)

    def gather_chip(s, h):
        to_sibling(s).wait_recv()
        total = pbuf[s, core, 1 - lo].astype(jnp.float32) + rbuf[s, 1 - lo].astype(jnp.float32)
        sbuf[s] = total.astype(jnp.bfloat16)
        to_pair(s).start()

    def gather_pair(s, h):
        to_pair(s).wait_recv()
        total = (
            pbuf[s, core, lo].astype(jnp.float32)
            + rbuf[s, lo].astype(jnp.float32)
            + ybuf[s].astype(jnp.float32)
        )
        fbuf[s] = total.astype(jnp.bfloat16)

        @pl.when(inner)
        def _():
            own_on(s).start()

        @pl.when(jnp.logical_and(x < 2, goes_left(s)))
        def _():
            own_left(s).start()

        @pl.when(row_end)
        def _():
            row_old(s, h).start()

    def chunk_taps(s):
        return taps[:, pl.ds(pl.multiple_of(s // 2 * LANES, LANES), LANES)]

    def frame(ref, s, at, f):
        return ref[s, at, f * LANES : (f + 1) * LANES].astype(jnp.float32)

    def pass_on(s, h):
        @pl.when(x > 0)
        def _():
            own_on(s).wait_recv()

        @pl.when(jnp.logical_and(jnp.logical_or(at1, at2), jnp.logical_not(goes_left(s))))
        def _():
            old_on(s).start()

        @pl.when(row_end)
        def _():
            weights = chunk_taps(s)
            at = slice(0, 2 * part_rows)
            window = [frame(pin, s, at, f) for f in range(1, frames)]
            window += [frame(fbuf, s, at, f) for f in range(frames)]
            for j in range(frames):
                total = weights[0:1] * window[j]
                for k in range(1, count - 1 - j):
                    total = total + weights[k : k + 1] * window[j + k]
                gbuf[s, at, j * LANES : (j + 1) * LANES] = total.astype(jnp.bfloat16)
            ahead_up(s, h).start()

    def relay_old(s, h):
        @pl.when(relays_old(h))
        def _():
            row_old(s, h).wait_recv()
            row_old_on(s, h).start()

        @pl.when(jnp.logical_and(jnp.logical_or(at0, at3), goes_left(s)))
        def _():
            own_left(s).wait_recv()
            left_on(s).start()

    def relay_ahead(s, h):
        @pl.when(relays_ahead(h))
        def _():
            ahead_up(s, h).wait_recv()
            ahead_on(s, h).start()

    def finish(s, h):
        @pl.when(row_start)
        def _():
            ahead_on(s, h).wait_recv()

        @pl.when(jnp.logical_or(fed, x > 1))
        def _():
            old_on(s).wait_recv()

        if h == 0:

            @pl.when(s == 0)
            def _():
                load_t.wait()

        weights = chunk_taps(s)

        @pl.when(at0)
        def _():
            base[...] = pin[s].astype(jnp.float32)

        @pl.when(x > 0)
        def _():
            at = slice(0, 2 * part_rows)
            window = [frame(qin, s, at, f) for f in range(frames - 1)]
            window += [frame(pin, s, at, f) for f in range(frames)]
            for j in range(frames):
                total = weights[0:1] * window[j]
                for k in range(1, count - 1 - j):
                    total = total + weights[k : k + 1] * window[j + k]
                base[at, j * LANES : (j + 1) * LANES] = total

        for p in range(2):
            at = slice(p * part_rows, (p + 1) * part_rows)
            window = [frame(fbuf, s, at, f) for f in range(frames)]
            for j in range(frames):
                total = base[at, j * LANES : (j + 1) * LANES]
                for f in range(j + 1):
                    k = count - 1 - j + f
                    total = total + weights[k : k + 1] * window[f]
                above = slice(j * part_rows, (j + 1) * part_rows)
                below = slice((frames + j) * part_rows, (frames + j + 1) * part_rows)
                value = total.astype(jnp.bfloat16)
                lhs[above, p * LANES : (p + 1) * LANES] = value
                if p == 0:
                    lhs[below, LANES:] = -value
                else:
                    lhs[below, :LANES] = value
        lines = slice(h * 2 * frames * part_rows, (h + 1) * 2 * frames * part_rows)
        for n in range(channels // 256):
            cols = slice(n * 256, (n + 1) * 256)
            piece = jnp.dot(lhs[...], tab[s // 2, :, cols], preferred_element_type=jnp.float32)

            @pl.when(s < 2)
            def _():
                out[lines, cols] = piece

            @pl.when(s >= 2)
            def _():
                out[lines, cols] += piece

    def drain(s, h):
        to_sibling(s).wait_send()
        to_pair(s).wait_send()

        @pl.when(inner)
        def _():
            own_on(s).wait_send()

        @pl.when(row_end)
        def _():
            row_old(s, h).wait_send()
            ahead_up(s, h).wait_send()

        @pl.when(relays_old(h))
        def _():
            row_old_on(s, h).wait_send()

        @pl.when(relays_ahead(h))
        def _():
            ahead_on(s, h).wait_send()

        @pl.when(jnp.logical_and(x < 2, goes_left(s)))
        def _():
            own_left(s).wait_send()

        @pl.when(jnp.logical_and(jnp.logical_or(at0, at3), goes_left(s)))
        def _():
            left_on(s).wait_send()

        @pl.when(jnp.logical_and(jnp.logical_or(at1, at2), jnp.logical_not(goes_left(s))))
        def _():
            old_on(s).wait_send()

    stages = [
        (0, form),
        (1, gather_chip),
        (3, gather_pair),
        (5, pass_on),
        (6, relay_old),
        (7, relay_ahead),
        (DRAIN_LAG, drain),
        (9, finish),
    ]
    load_k.wait()

    def turn(k, carry):
        for now in range(2):
            for lag, stage in stages:
                s = 2 * k + now - lag

                @pl.when(jnp.logical_and(s >= 0, s < 2 * steps))
                def _():
                    stage(s, (now - lag) % 2)

        return carry

    turns = steps + (stages[-1][0] + 1) // 2
    lax.fori_loop(0, turns, turn, 0)

    def settle(c, carry):
        for h in range(2):
            drain(2 * c + h, h)
        return carry

    lax.fori_loop((turns * 2 - DRAIN_LAG) // 2, steps, settle, 0)


def spread(rows, out, sem):
    owned, frames = out.shape[:2]
    half = owned // 2
    copies = []
    for h in range(2):
        for part in range(2):
            for f in range(frames):
                at = ((h * 2 + part) * frames + f) * half
                to = out.at[pl.ds(h * half, half), f, part]
                copies.append(
                    pltpu.make_async_copy(rows.at[pl.ds(at, half)], to, sem.at[h, part, f])
                )
    for copy in copies:
        copy.start()
    for copy in copies:
        copy.wait()


def body(samples, weights, filter_taps):
    depth, span = samples.shape[1:]
    owned = weights.shape[2] // lax.axis_size("inp")
    channels = filter_taps.shape[1]
    frames = span // channels
    steps = channels // LANES
    width = frames * LANES
    old = width - LANES
    table = jnp.asarray(transform_table(channels))
    half = jnp.bfloat16
    dma = pltpu.SemaphoreType.DMA
    rows = 2 * owned
    units = 2 * steps
    anywhere = pl.BlockSpec(memory_space=pltpu.HBM)
    inside = pl.BlockSpec(memory_space=pltpu.VMEM)
    lines = pl.pallas_call(
        functools.partial(kernel, steps, frames),
        out_shape=jax.ShapeDtypeStruct((2 * frames * owned, channels), jnp.float32),
        in_specs=[anywhere] * 4,
        out_specs=inside,
        scratch_shapes=[
            pltpu.VMEM((steps, 2, depth, width), half),
            pltpu.VMEM(weights.shape, half),
            pltpu.VMEM(filter_taps.shape, jnp.float32),
            pltpu.VMEM(table.shape, half),
            pltpu.VMEM((2, 2 * rows, 2 * depth), half),
            pltpu.VMEM((units, 2, 2, owned, width), half),
            pltpu.VMEM((units, 2, owned, width), half),
            pltpu.VMEM((units, owned, width), half),
            pltpu.VMEM((units, owned, width), half),
            pltpu.VMEM((units, owned, width), half),
            pltpu.VMEM((units, owned, width), half),
            pltpu.VMEM((units, owned, old), half),
            pltpu.VMEM((units, owned, old), half),
            pltpu.VMEM((units, owned, old), half),
            pltpu.VMEM((units, owned, width), half),
            pltpu.VMEM((units, owned, width), half),
            pltpu.VMEM((owned, width), jnp.float32),
            pltpu.VMEM((frames * owned, 2 * LANES), half),
            dma((steps, frames)),
            dma,
            dma,
            dma,
            dma((units,)),
            dma((units,)),
            dma((units,)),
            dma((units,)),
            dma((units,)),
            dma((units,)),
            dma((units,)),
            dma((units,)),
            dma((units,)),
            dma((units,)),
            dma((units,)),
            dma((units,)),
            dma((units,)),
            dma((units,)),
            dma((units,)),
            dma((units,)),
            dma((units,)),
        ],
        compiler_params=pltpu.CompilerParams(
            collective_id=0, has_side_effects=True, vmem_limit_bytes=61 << 20
        ),
        name="beams",
    )(samples, weights, filter_taps, table)
    return pl.pallas_call(
        spread,
        out_shape=jax.ShapeDtypeStruct((owned, frames, 2, channels), jnp.float32),
        in_specs=[inside],
        out_specs=pl.BlockSpec(memory_space=pltpu.HBM),
        scratch_shapes=[dma((2, 2, frames))],
        name="spread",
    )(lines)


def solution(mesh):
    return jax.shard_map(
        body,
        mesh=mesh,
        in_specs=(P(None, "inp", "tm"), P(None, "inp", None), P()),
        out_specs=P("inp", "tm", None, None),
        check_vma=False,
    )
```
